256 devices in a mesh: example: 32 (over z_hi, x, core), tensor: 8 (over z_lo, y).
Axes of the slice: x: 4, y: 4, z: 8 (z_hi: 4, z_lo: 2; z = z_hi * 2 + z_lo), core: 2. Of those that a mesh axis runs over, the one named last changes fastest.
Arguments:
- layer_input: bfloat16 [16384, 4096], P('example', 'tensor'), may hold values from -6 to 6
- gate_act: bfloat16 [16384, 14336], P('example', 'tensor'), may hold values from -8 to 8
- hidden_grad: bfloat16 [16384, 14336], P('example', 'tensor'), may hold values from -6 to 6
- up_weight: bfloat16 [4096, 14336], P('example', 'tensor'), may hold values from -0.046875 to 0.046875
- proj_input: bfloat16 [4096, 64], P('tensor'), may hold values from -0.09375 to 0.09375
- proj_output: bfloat16 [14336, 64], P('tensor'), may hold values from -0.046875 to 0.046875
- sequence_ids: int32 [16384], P('example'), may hold values from 0 to 127, as said below
Outputs:
- input_grad: bfloat16 [16384, 4096], P('example', 'tensor')
- features: float32 [128, 4096], P('example')
- hessian: float32 [4096, 4096], P('example', 'tensor')
The draws below stay inside these ranges and needn't reach their ends.
Inputs may be any that keep to these rules, and one draw needn't show every extreme that they name: `sequence_ids`: token block b (tokens b * 512 to (b + 1) * 512 - 1) holds exactly the 4 examples b * 4 to (b + 1) * 4 - 1, each a run of one or more tokens, in order; the first token of a block starts its first example.
All inputs are finite; a program needn't handle non-finite values.
Results may differ from the reference program's by a relative error of at most 0.0049.
Values may be sent and summed in bfloat16 or wider, within the bound.
A program may use at most 128 MiB of HBM per device.

```python
import jax
import jax.numpy as jnp
from jax import lax

D = 4096
FF = 14336
RANK = 64
TOK_DEV = 512
SEQS_DEV = 4
TOKENS = 16384
EXAMPLES = 128
N_EXAMPLE = 32


def draw_sequence_ids(key, part):
    key = jax.random.fold_in(key, 7)
    blocks = TOKENS // TOK_DEV
    block_keys = jax.random.split(key, blocks)
    orders = jax.vmap(lambda single: jax.random.permutation(single, TOK_DEV - 1))(block_keys)
    cut_points = orders[:, :SEQS_DEV - 1].astype(jnp.int32) + 1
    position = jnp.arange(TOK_DEV, dtype=jnp.int32)
    local_ids = jnp.sum((position[None, :, None] >= cut_points[:, None, :]).astype(jnp.int32), axis=2)
    offsets = jnp.arange(blocks, dtype=jnp.int32) * SEQS_DEV
    return (local_ids + offsets[:, None]).reshape(TOKENS).astype(jnp.int32)


def block_levels(key, dims, cuts, smallest, high):
    level, own = 1.0, jax.random.fold_in(key, 6)
    for dim, blocks in cuts:
        steps = jnp.exp(jax.random.uniform(jax.random.fold_in(own, dim), (blocks,), jnp.float32, smallest / len(cuts), high / len(cuts)))
        level = level * jnp.repeat(steps, dims[dim] // blocks).reshape([-1 if axis == dim else 1 for axis in range(len(dims))])
    return level


def normal_values(rng, shape, scale, bound, shards=(), kind=jnp.bfloat16):
    values = jax.random.normal(rng, shape, jnp.float32) * scale
    if len(shards) > 0:
        values = block_levels(rng, shape, shards, -0.22, 0.18) * values
    return jnp.clip(values, min=-bound, max=bound).astype(kind)


def setup_inputs(seed: int = 0) -> dict:
    keys = jax.random.split(jax.random.key(seed), 8)
    return {
        "layer_input": normal_values(keys[0], (TOKENS, D), 1.0, 6.0, ((0, 32), (1, 8))),
        "gate_act": normal_values(keys[1], (TOKENS, FF), 1.5, 8.0, ((0, 32), (1, 8))),
        "hidden_grad": normal_values(keys[2], (TOKENS, FF), 1.0, 6.0, ((0, 32), (1, 8))),
        "up_weight": normal_values(keys[3], (D, FF), FF ** -0.5, 0.046875, ((0, 32), (1, 8))),
        "proj_input": normal_values(keys[4], (D, RANK), D ** -0.5, 0.09375, ((0, 8),)),
        "proj_output": normal_values(keys[5], (FF, RANK), FF ** -0.5, 0.046875, ((0, 8),)),
        "sequence_ids": draw_sequence_ids(jax.random.fold_in(keys[7], 71), 0),
    }


damping = 0.1


def block_features(blocks):
    input_rows, up_rows, id_rows, proj_input, proj_output = blocks
    input_low = jnp.dot(input_rows, proj_input, preferred_element_type=jnp.float32)
    output_low = jnp.dot(up_rows, proj_output, preferred_element_type=jnp.float32)
    local_ids = id_rows - id_rows[0]
    onehot = (local_ids[:, None] == jnp.arange(SEQS_DEV, dtype=jnp.int32)[None, :]).astype(jnp.float32)
    weighted = (onehot[:, :, None] * input_low[:, None, :]).reshape(TOK_DEV, SEQS_DEV * RANK)
    grads = jnp.dot(weighted.T, output_low, precision=lax.Precision.HIGHEST, preferred_element_type=jnp.float32)
    return grads.reshape(SEQS_DEV, RANK * RANK) * ((SEQS_DEV / TOK_DEV) ** 0.5)


def reference(layer_input, gate_act, hidden_grad, up_weight, proj_input, proj_output, sequence_ids):
    up_grad = (hidden_grad.astype(jnp.float32) * jax.nn.silu(gate_act.astype(jnp.float32))).astype(jnp.bfloat16)
    input_grad = jnp.dot(up_grad, up_weight.T, preferred_element_type=jnp.float32).astype(jnp.bfloat16)
    inputs_blocked = layer_input.reshape(N_EXAMPLE, TOK_DEV, D)
    up_blocked = up_grad.reshape(N_EXAMPLE, TOK_DEV, FF)
    ids_blocked = sequence_ids.reshape(N_EXAMPLE, TOK_DEV)
    features = lax.map(lambda pair: block_features((pair[0], pair[1], pair[2], proj_input, proj_output)), (inputs_blocked, up_blocked, ids_blocked))
    features = features.reshape(EXAMPLES, RANK * RANK)
    hessian = jnp.dot(features.T, features, precision=lax.Precision.HIGHEST, preferred_element_type=jnp.float32) / EXAMPLES
    hessian = hessian + damping * jnp.eye(RANK * RANK, dtype=jnp.float32)
    return input_grad, features, hessian
```

```python
import jax
import jax.numpy as jnp
from jax import lax
from jax.experimental import pallas as pl
from jax.experimental.pallas import tpu as pltpu
from jax.sharding import PartitionSpec as P

MESH = pl.DeviceIdType.MESH
F32 = jnp.float32
BF16 = jnp.bfloat16
HIGHEST = lax.Precision.HIGHEST

DAMPING = 0.1
TOK = 512
KDIM = 1792
RANK = 64
ROUNDS = 4
ROWS = 32
PAIR_TILES = [[(i, a) for a in range(i + 1)] + [(r, i) for r in range(i)] for i in range(ROUNDS)]
NT = [4 + len(PAIR_TILES[i]) for i in range(ROUNDS)]


class Copies:
    def __init__(self, send_sems, recv_sems):
        self.send, self.recv, self.count, self.sent = send_sems, recv_sems, 0, []

    def make(self, src, dst, device):
        index = self.count
        self.count += 1
        copy = pltpu.make_async_remote_copy(
            src_ref=src,
            dst_ref=dst,
            send_sem=self.send.at[index],
            recv_sem=self.recv.at[index],
            device_id=device,
            device_id_type=MESH,
        )
        return copy

    def go(self, src, dst, device):
        copy = self.make(src, dst, device)
        copy.start()
        self.sent.append(copy)
        return copy


N_COPIES = 192


def kernel(
    x_in, gate_in, hid_in, w_in, pi_in, po_in, ids_ref,
    o_ref, feat_ref, hess_ref,
    xv, gv, hv, piv, pov, a_own, a_pair, wbuf,
    sb0, sb1, sb2, sb3, r1p, r1m, r2m, r2p, zs, zr, sown, xs, xr,
    low, lowr, fpart, fpr, fmine, fsib, gcol, rowb,
    send_sems, recv_sems, loc_sems,
):
    e = lax.axis_index("example")
    t = lax.axis_index("tensor")
    zh, x, c = e // 8, (e // 2) % 4, e % 2
    zl, y = t // 4, t % 4

    def ex(zh_, x_, c_):
        return zh_ * 8 + x_ * 2 + c_

    def te(zl_, y_):
        return zl_ * 4 + y_

    sib = (ex(zh, x, 1 - c), t)
    pair = (ex(zh, x + 1 - 2 * (x % 2), c), t)
    qdev = (ex(zh, 3 - x, c), t)
    zp = (ex((zh + 1) % 4, x, c), t)
    zm = (ex((zh + 3) % 4, x, c), t)
    yp = (e, te(zl, (y + 1) % 4))
    ym = (e, te(zl, (y + 3) % 4))
    zlp = (e, te(1 - zl, y))
    xs_dev = {dx: (ex(zh, (x + dx) % 4, c), t) for dx in (1, 2, 3)}
    zs_dev = {dz: (ex((zh + dz) % 4, x, c), t) for dz in (1, 2, 3)}
    tens = [(dzl, dy) for dzl in range(2) for dy in range(4) if (dzl, dy) != (0, 0)]
    tidx = {d: te((zl + d[0]) % 2, (y + d[1]) % 4) for d in tens}

    barrier = pltpu.get_barrier_semaphore()
    partners = [sib] + list(xs_dev.values()) + list(zs_dev.values()) + [(e, tidx[d]) for d in tens]
    for dev in partners:
        pl.semaphore_signal(barrier, inc=1, device_id=dev, device_id_type=MESH)

    loads = []

    def load(src, dst):
        copy = pltpu.make_async_copy(src, dst, loc_sems.at[len(loads)])
        copy.start()
        loads.append(copy)
        return copy

    w_load = [load(w_in.at[pl.ds(r * ROWS, ROWS)], wbuf.at[r, 0, c]) for r in range(ROUNDS)]
    gh_load = []
    for a in range(4):
        rows = pl.ds(a * 128, 128)
        gh_load.append((load(gate_in.at[rows], gv.at[rows]), load(hid_in.at[rows], hv.at[rows])))
    low_load = [load(x_in, xv), load(pi_in, piv), load(po_in, pov)]

    pl.semaphore_wait(barrier, len(partners))
    cp = Copies(send_sems, recv_sems)

    def slot(r, dz, s, core):
        return wbuf.at[r, (dz % 2) * 2 + s, (dz // 2) * 2 + core]

    w_z = {}
    w_x = {}
    w_s = {}

    def own_sends(r):
        w_load[r].wait()
        w_z[r, 3] = cp.go(slot(r, 0, 0, c), slot(r, 3, 0, c), zp)
        w_z[r, 1] = cp.go(slot(r, 0, 0, c), slot(r, 1, 0, c), zm)
        w_x[r, 0] = cp.go(slot(r, 0, 0, c), slot(r, 0, 1, c), qdev)
        w_s[r, 0, 0] = cp.go(slot(r, 0, 0, c), slot(r, 0, 0, c), sib)

    def s1(r):
        w_z[r, 3].wait_recv()
        half = pl.ds(0, ROWS // 2)
        w_z[r, "2a"] = cp.go(slot(r, 3, 0, c).at[half], slot(r, 2, 0, c).at[half], zp)
        w_x[r, 3] = cp.go(slot(r, 3, 0, c), slot(r, 3, 1, c), qdev)
        w_s[r, 3, 0] = cp.go(slot(r, 3, 0, c), slot(r, 3, 0, c), sib)
        w_z[r, 1].wait_recv()
        half = pl.ds(ROWS // 2, ROWS // 2)
        w_z[r, "2b"] = cp.go(slot(r, 1, 0, c).at[half], slot(r, 2, 0, c).at[half], zm)
        w_x[r, 1] = cp.go(slot(r, 1, 0, c), slot(r, 1, 1, c), qdev)
        w_s[r, 1, 0] = cp.go(slot(r, 1, 0, c), slot(r, 1, 0, c), sib)
        if r + 2 < ROUNDS:
            own_sends(r + 2)

    def s2(r):
        w_z[r, "2a"].wait_recv()
        w_z[r, "2b"].wait_recv()
        w_x[r, 2] = cp.go(slot(r, 2, 0, c), slot(r, 2, 1, c), qdev)
        w_s[r, 2, 0] = cp.go(slot(r, 2, 0, c), slot(r, 2, 0, c), sib)

    def s3(r):
        for dz in (0, 3, 1, 2):
            w_x[r, dz].wait_recv()
            w_s[r, dz, 1] = cp.go(slot(r, dz, 1, c), slot(r, dz, 1, c), sib)

    def s4(r):
        for dz in (0, 3, 1, 2):
            for s in range(2):
                w_s[r, dz, s].wait_recv()

    own_sends(0)
    own_sends(1)

    a_copy = []
    for a in range(4):
        for copy in gh_load[a]:
            copy.wait()

        def up(j, _, a=a):
            rows = pl.ds(a * 128 + j * 16, 16)
            g = gv[rows].astype(F32)
            h = hv[rows].astype(F32)
            a_own[rows] = (h * (g / (1.0 + jnp.exp(-g)))).astype(BF16)
            return 0

        lax.fori_loop(0, 8, up, 0)
        rows = pl.ds(a * 128, 128)
        a_copy.append(cp.go(a_own.at[rows], a_pair.at[rows], pair))

    for copy in low_load:
        copy.wait()
    for n in range(4):
        rows = pl.ds(n * 128, 128)
        one = jnp.dot(xv[rows], piv[...], preferred_element_type=F32)
        two = jnp.dot(a_own[rows], pov[...], preferred_element_type=F32)
        both = jnp.concatenate([one, two], axis=1)
        low[2 * n] = both[:64]
        low[2 * n + 1] = both[64:]
    l2 = [cp.go(low.at[tidx[d]], lowr.at[i], (e, tidx[d])) for i, d in enumerate(tens)]
    lc = {}

    def l3():
        total = low[t]
        for i in range(7):
            l2[i].wait_recv()
            total = total + lowr[i]
        lane = lax.broadcasted_iota(jnp.int32, (64, 128), 1)
        out2 = jnp.where(lane < 64, pltpu.roll(total, 64, 1), total)
        out8 = jnp.concatenate([out2] * 4, axis=1)
        local = ids_ref[pl.ds(t, 1), :] - 4 * e + 4 * c
        hot = (lax.broadcasted_iota(jnp.int32, (8, 64), 0) == local).astype(F32)
        hot = hot * ((4 / 512) ** 0.5)

        def piece(j, _):
            spread = (
                lax.broadcasted_iota(jnp.int32, (128, 512), 0)
                == lax.broadcasted_iota(jnp.int32, (128, 512), 1) // 64 + 8 * j
            ).astype(F32)
            rep = jnp.dot(total, spread, precision=HIGHEST, preferred_element_type=F32)
            fpart[j] = jnp.dot(hot, rep * out8, precision=HIGHEST, preferred_element_type=F32)
            return 0

        lax.fori_loop(0, 8, piece, 0)
        lc["f"] = [cp.go(fpart.at[tidx[d]], fpr.at[i], (e, tidx[d])) for i, d in enumerate(tens)]

    def l4():
        total = fpart[t]
        for i in range(7):
            lc["f"][i].wait_recv()
            total = total + fpr[i]
        fmine[...] = total
        feat_ref[t] = total
        lc["sib"] = cp.go(fmine, fsib, sib)
        lc["out"] = [cp.go(fmine, feat_ref.at[t], (e, tidx[d])) for d in tens]

    def l5():
        lc["sib"].wait_recv()
        gcol[0, 0] = fmine[...] + fsib[...]
        lc["x"] = [cp.go(gcol.at[0, 0], gcol.at[0, dx], xs_dev[dx]) for dx in (1, 2, 3)]

    def l6():
        for copy in lc["x"]:
            copy.wait_recv()
        lc["z"] = [cp.go(gcol.at[0], gcol.at[dz], zs_dev[dz]) for dz in (1, 2, 3)]

    def l7():
        for copy in lc["z"]:
            copy.wait_recv()
        lanes = pl.ds(pl.multiple_of((e % 4) * 128, 128), 128)
        rowb[0] = gcol[:, :, :, lanes]
        index = cp.count
        cp.count += 8
        lc["row"] = [
            pltpu.make_async_remote_copy(
                src_ref=rowb.at[0],
                dst_ref=rowb.at[1],
                send_sem=send_sems.at[index + i],
                recv_sem=recv_sems.at[index],
                device_id=(e, tidx[d]),
                device_id_type=MESH,
            )
            for i, d in enumerate(tens)
        ]

        @pl.when(t == e // 4)
        def _():
            for copy in lc["row"]:
                copy.start()
            rowb[1] = rowb[0]

    def l8():
        @pl.when(t == e // 4)
        def _():
            for copy in lc["row"]:
                copy.wait_send()

        @pl.when(t != e // 4)
        def _():
            lc["row"][0].wait_recv()

        row = rowb[1].reshape(128, 128)
        col = gcol[...].reshape(128, 512)
        gram = jnp.dot(row.T, col, precision=HIGHEST, preferred_element_type=F32) / 128.0
        rg = lax.broadcasted_iota(jnp.int32, (128, 512), 0) + e * 128
        cg = lax.broadcasted_iota(jnp.int32, (128, 512), 1) + t * 512
        hess_ref[...] = gram + DAMPING * (rg == cg).astype(F32)

    sb = [sb0, sb1, sb2, sb3]

    def kslot(yy):
        return ((yy // 2 + zh) % 2) * 2 + (yy % 2 + x // 2) % 2

    k0, kp, km, k2 = (kslot((y + d) % 4) for d in (0, 1, 3, 2))
    base = ((zh + k0 // 2) % 4) // 2
    h_own = (zl + base) % 2
    h_oth = 1 - h_own
    par = (y + x // 2 + x) % 2
    off = [sum(NT[:i]) for i in range(ROUNDS)]
    poff = [sum(len(q) for q in PAIR_TILES[:i]) for i in range(ROUNDS)]
    c1c, c2c, zc, xc = {}, {}, {}, {}

    def put(i, res, first):
        count = res.shape[1] // 128
        for k in range(4):
            for h in range(2):
                for n in range(count):
                    row0 = (k * 2 + h) * 64
                    sb[i][k, h, first + n] = res[row0 : row0 + 64, n * 128 : n * 128 + 128].astype(BF16)

    def mm(r, a_ref, rows):
        return lax.dot_general(
            wbuf[r].reshape(512, KDIM), a_ref[rows], (((1,), (1,)), ((), ())), preferred_element_type=F32
        )

    def compute(i):
        for half in range(2):
            put(i, mm(i, a_own, pl.ds(half * 256, 256)), half * 2)
        a_copy[i].wait_recv()
        for n, (r, a) in enumerate(PAIR_TILES[i]):
            put(i, mm(r, a_pair, pl.ds(a * 128, 128)), 4 + n)

    def c1(i):
        span = pl.ds(off[i], NT[i])
        c1c[i, "p"] = cp.go(sb[i].at[k2, 0], r1p.at[span], yp)
        c1c[i, "m"] = cp.go(sb[i].at[k2, 1], r1m.at[span], ym)
        c2c[i, "p1"] = cp.go(sb[i].at[kp, 1], r2m.at[1, span], yp)
        c2c[i, "m0"] = cp.go(sb[i].at[km, 0], r2p.at[0, span], ym)

    def c2(i):
        span = pl.ds(off[i], NT[i])
        c1c[i, "p"].wait_recv()
        sb[i][kp, 0] = (sb[i][kp, 0].astype(F32) + r1p[span].astype(F32)).astype(BF16)
        c2c[i, "p0"] = cp.go(sb[i].at[kp, 0], r2m.at[0, span], yp)
        c1c[i, "m"].wait_recv()
        sb[i][km, 1] = (sb[i][km, 1].astype(F32) + r1m[span].astype(F32)).astype(BF16)
        c2c[i, "m1"] = cp.go(sb[i].at[km, 1], r2p.at[1, span], ym)

    def c3(i):
        span = pl.ds(off[i], NT[i])
        for name in ("p1", "m0", "p0", "m1"):
            c2c[i, name].wait_recv()

        def total(h):
            return sb[i][k0, h].astype(F32) + r2m[h, span].astype(F32) + r2p[h, span].astype(F32)

        zs[span] = total(h_oth).astype(BF16)
        zc[i] = cp.go(zs.at[span], zr.at[span], zlp)
        sown[span] = total(h_own)

    def c4(i):
        zc[i].wait_recv()
        for n in range(4):
            done = (sown[off[i] + n] + zr[off[i] + n].astype(F32)).astype(BF16)
            o_ref[par, 0, i, :, n * 128 : n * 128 + 128] = done[:ROWS]
            o_ref[par, 1, i, :, n * 128 : n * 128 + 128] = done[ROWS:]
        count = len(PAIR_TILES[i])
        src = pl.ds(off[i] + 4, count)
        span = pl.ds(poff[i], count)
        xs[span] = (sown[src] + zr[src].astype(F32)).astype(BF16)
        xc[i] = cp.go(xs.at[span], xr.at[span], pair)

    def c5(i):
        xc[i].wait_recv()
        for n, (r, a) in enumerate(PAIR_TILES[i]):
            done = xr[poff[i] + n]
            o_ref[1 - par, 0, r, :, a * 128 : a * 128 + 128] = done[:ROWS]
            o_ref[1 - par, 1, r, :, a * 128 : a * 128 + 128] = done[ROWS:]

    s1(0)
    l3()
    s2(0)
    s3(0)
    s1(1)
    s4(0)
    compute(0)
    c1(0)
    l4()
    s2(1)
    s3(1)
    c2(0)
    s1(2)
    s4(1)
    compute(1)
    c1(1)
    l5()
    c3(0)
    s2(2)
    s3(2)
    c2(1)
    s1(3)
    s4(2)
    compute(2)
    c1(2)
    l6()
    c4(0)
    c3(1)
    s2(3)
    c2(2)
    s3(3)
    s4(3)
    compute(3)
    c1(3)
    l7()
    c4(1)
    c3(2)
    c2(3)
    l8()
    c4(2)
    c3(3)
    c5(0)
    c5(1)
    c4(3)
    c5(2)
    for copy in lc["out"]:
        copy.wait_recv()
    for copy in cp.sent:
        copy.wait_send()
    c5(3)


def body(layer_input, gate_act, hidden_grad, up_weight, proj_input, proj_output, sequence_ids):
    tiles = sum(NT)
    pair_tiles = sum(len(q) for q in PAIR_TILES)
    anyspec = pl.BlockSpec(memory_space=pl.ANY)
    vm = pl.BlockSpec(memory_space=pltpu.VMEM)
    o, feat, hess = pl.pallas_call(
        kernel,
        out_shape=(
            jax.ShapeDtypeStruct((2, 2, ROUNDS, ROWS, TOK), BF16),
            jax.ShapeDtypeStruct((8, 8, 512), F32),
            jax.ShapeDtypeStruct((128, 512), F32),
        ),
        in_specs=[anyspec] * 6 + [vm],
        out_specs=(vm, vm, vm),
        scratch_shapes=[
            pltpu.VMEM((512, 512), BF16),
            pltpu.VMEM((512, KDIM), BF16),
            pltpu.VMEM((512, KDIM), BF16),
            pltpu.VMEM((512, RANK), BF16),
            pltpu.VMEM((KDIM, RANK), BF16),
            pltpu.VMEM((512, KDIM), BF16),
            pltpu.VMEM((512, KDIM), BF16),
            pltpu.VMEM((ROUNDS, 4, 4, ROWS, KDIM), BF16),
        ]
        + [pltpu.VMEM((4, 2, NT[i], 64, 128), BF16) for i in range(ROUNDS)]
        + [
            pltpu.VMEM((tiles, 64, 128), BF16),
            pltpu.VMEM((tiles, 64, 128), BF16),
            pltpu.VMEM((2, tiles, 64, 128), BF16),
            pltpu.VMEM((2, tiles, 64, 128), BF16),
            pltpu.VMEM((tiles, 64, 128), BF16),
            pltpu.VMEM((tiles, 64, 128), BF16),
            pltpu.VMEM((tiles, 64, 128), F32),
            pltpu.VMEM((pair_tiles, 64, 128), BF16),
            pltpu.VMEM((pair_tiles, 64, 128), BF16),
            pltpu.VMEM((8, 64, 128), F32),
            pltpu.VMEM((7, 64, 128), F32),
            pltpu.VMEM((8, 8, 512), F32),
            pltpu.VMEM((7, 8, 512), F32),
            pltpu.VMEM((8, 512), F32),
            pltpu.VMEM((8, 512), F32),
            pltpu.VMEM((4, 4, 8, 512), F32),
            pltpu.VMEM((2, 4, 4, 8, 128), F32),
            pltpu.SemaphoreType.DMA((N_COPIES,)),
            pltpu.SemaphoreType.DMA((N_COPIES,)),
            pltpu.SemaphoreType.DMA((16,)),
        ],
        compiler_params=pltpu.CompilerParams(
            collective_id=0, has_side_effects=True, vmem_limit_bytes=60 * 1024 * 1024
        ),
    )(layer_input, gate_act, hidden_grad, up_weight, proj_input, proj_output, sequence_ids.reshape(8, 64))
    input_grad = o.reshape(512, TOK).T
    features = (feat[:, :4] + feat[:, 4:]).transpose(1, 0, 2).reshape(4, 4096)
    return input_grad, features, hess


def solution(mesh):
    return jax.shard_map(
        body,
        mesh=mesh,
        in_specs=(
            P("example", "tensor"),
            P("example", "tensor"),
            P("example", "tensor"),
            P("example", "tensor"),
            P("tensor", None),
            P("tensor", None),
            P("example"),
        ),
        out_specs=(P("example", "tensor"), P("example", None), P("example", "tensor")),
        check_vma=False,
    )
```

```python
import jax
import jax.numpy as jnp
from jax import lax
from jax.experimental import pallas as pl
from jax.experimental.pallas import tpu as pltpu
from jax.sharding import PartitionSpec as P

MESH = pl.DeviceIdType.MESH
F32 = jnp.float32
BF16 = jnp.bfloat16
LAST = (((1,), (1,)), ((), ()))
HIGHEST = lax.Precision.HIGHEST

DAMPING = 0.1
TOK = 512
KDIM = 1792
RANK = 64
ROUNDS = 8
ROWS = 16
SUB = 2 * ROWS
OWN_X, OWN_Z = 8, 3
PLAN = (
    ("0o", "00"),
    ("1o", "10"),
    ("2o", "20", "21", "01", "11"),
    ("3o", "30", "31"),
    ("4o", "40", "41", "42", "02", "12", "22", "32"),
    ("5o", "50", "51", "52"),
    ("03", "13", "23", "33", "43", "53"),
    ("6o", "60", "61", "62", "63"),
    ("7o", "70", "71", "72", "73"),
)


def tiles_of(text):
    own, other = [], []
    for word in text:
        if word[1] == "o":
            own += [("own", int(word[0]), n) for n in range(4)]
        else:
            other.append(("pair", int(word[0]), int(word[1])))
    return own, other


OWNS = [tiles_of(text)[0] for text in PLAN]
PAIRS = [tiles_of(text)[1] for text in PLAN]
BATCHES = [o + p for o, p in zip(OWNS, PAIRS)]
NB = len(BATCHES)
LATE = 8
NT = [len(q) for q in BATCHES]
NP = [len(q) for q in PAIRS]

STEPS = (
    "s10", "s11", "l2", "s20", "s12", "l3", "s30", "s21", "s13", "s40", "mm0", "c10",
    "l4", "s31", "s22", "s14", "s41", "mm1", "c11", "c20", "l5", "s32", "s23", "s15",
    "s42", "mm2", "c12", "c21", "l6", "s33", "s24", "s16", "s43", "mm3", "c13", "c22",
    "c30", "l7", "s34", "s25", "s17", "s44", "mm4", "c14", "c23", "c31", "l8", "s26",
    "s35", "s45", "mm5", "c15", "c24", "c32", "l9", "s27", "mm6", "c16", "c25", "c33",
    "c40", "c41", "s36", "s46", "mm7", "c17", "c26", "c34", "c42", "c43", "s37", "c35",
    "c44", "s47", "mm8", "c18", "c27", "c36", "c45", "c28", "c37", "c46", "c38", "c47",
    "c50", "c51", "c52", "c53", "c54", "c55", "c56", "c57", "c48", "la", "c58",
)


class Copies:
    def __init__(self, send_sems, recv_sems):
        self.send, self.recv, self.count, self.sent = send_sems, recv_sems, 0, []

    def make(self, src, dst, device):
        index = self.count
        self.count += 1
        copy = pltpu.make_async_remote_copy(
            src_ref=src,
            dst_ref=dst,
            send_sem=self.send.at[index],
            recv_sem=self.recv.at[index],
            device_id=device,
            device_id_type=MESH,
        )
        return copy

    def go(self, src, dst, device):
        copy = self.make(src, dst, device)
        copy.start()
        self.sent.append(copy)
        return copy


N_COPIES = 300


def kernel(
    x_in, gate_in, hid_in, w_in, pi_in, po_in, ids_ref,
    o_ref, feat_ref, gcol, rowb,
    xv, gv, hv, piv, pov, a_own, a_pair, wbuf,
    sb, r1p, r1m, r2m, r2p, zs, zr, sown, xs, xr, xr2,
    low, lowr, lowz, fpart, fpr, fz, fsib,
    send_sems, recv_sems, loc_sems,
):
    e = lax.axis_index("example")
    t = lax.axis_index("tensor")
    zh, x, c = e // 8, (e // 2) % 4, e % 2
    zl, y = t // 4, t % 4

    def ex(zh_, x_, c_):
        return zh_ * 8 + x_ * 2 + c_

    def te(zl_, y_):
        return zl_ * 4 + y_

    sib = (ex(zh, x, 1 - c), t)
    pair = (ex(zh, x + 1 - 2 * (x % 2), c), t)
    pairz = (ex(zh, x + 1 - 2 * (x % 2), c), te(1 - zl, y))
    qdev = (ex(zh, 3 - x, c), t)
    zp = (ex((zh + 1) % 4, x, c), t)
    zm = (ex((zh + 3) % 4, x, c), t)
    yp = (e, te(zl, (y + 1) % 4))
    ym = (e, te(zl, (y + 3) % 4))
    zlp = (e, te(1 - zl, y))
    xs_dev = {dx: (ex(zh, (x + dx) % 4, c), t) for dx in (1, 2, 3)}
    zs_dev = {dz: (ex((zh + dz) % 4, x, c), t) for dz in (1, 2, 3)}
    y_dev = {d: (e, te(zl, (y + d) % 4)) for d in (1, 2, 3)}
    tens = [(dzl, dy) for dzl in range(2) for dy in range(4) if (dzl, dy) != (0, 0)]
    tidx = {d: te((zl + d[0]) % 2, (y + d[1]) % 4) for d in tens}

    barrier = pltpu.get_barrier_semaphore()
    partners = [sib, pairz] + list(xs_dev.values()) + list(zs_dev.values()) + [(e, tidx[d]) for d in tens]
    for dev in partners:
        pl.semaphore_signal(barrier, inc=1, device_id=dev, device_id_type=MESH)

    loads = []

    def load(src, dst):
        copy = pltpu.make_async_copy(src, dst, loc_sems.at[len(loads)])
        copy.start()
        loads.append(copy)
        return copy

    w_load = [load(w_in.at[pl.ds(r * ROWS, ROWS)], wbuf.at[r, 0, c]) for r in range(ROUNDS)]
    gh_load = []
    for a in range(4):
        rows = pl.ds(a * 128, 128)
        gh_load.append((load(gate_in.at[rows], gv.at[rows]), load(hid_in.at[rows], hv.at[rows])))
    low_load = [load(x_in, xv), load(pi_in, piv), load(po_in, pov)]

    pl.semaphore_wait(barrier, len(partners))
    cp = Copies(send_sems, recv_sems)

    def slot(r, dz, s, core):
        return wbuf.at[r, (dz % 2) * 2 + s, (dz // 2) * 2 + core]

    w_z = {}
    w_x = {}
    w_s = {}

    def own_z(r):
        if r < ROUNDS:
            w_z[r, 3] = cp.go(slot(r, 0, 0, c), slot(r, 3, 0, c), zp)
            w_z[r, 1] = cp.go(slot(r, 0, 0, c), slot(r, 1, 0, c), zm)

    def own_x(r):
        if r < ROUNDS:
            w_x[r, 0] = cp.go(slot(r, 0, 0, c), slot(r, 0, 1, c), qdev)

    def own_s(r):
        w_s[r, 0, 0] = cp.go(slot(r, 0, 0, c), slot(r, 0, 0, c), sib)

    def s1(r):
        w_z[r, 3].wait_recv()
        if r % 2 == 0:
            w_z[r, 2] = cp.go(slot(r, 3, 0, c), slot(r, 2, 0, c), zp)
        w_x[r, 3] = cp.go(slot(r, 3, 0, c), slot(r, 3, 1, c), qdev)
        w_z[r, 1].wait_recv()
        if r % 2 == 1:
            w_z[r, 2] = cp.go(slot(r, 1, 0, c), slot(r, 2, 0, c), zm)
        w_x[r, 1] = cp.go(slot(r, 1, 0, c), slot(r, 1, 1, c), qdev)
        own_z(r + OWN_Z)
        own_x(r + OWN_X)
        w_s[r, 3, 0] = cp.go(slot(r, 3, 0, c), slot(r, 3, 0, c), sib)
        w_s[r, 1, 0] = cp.go(slot(r, 1, 0, c), slot(r, 1, 0, c), sib)

    def s2(r):
        w_z[r, 2].wait_recv()
        w_x[r, 2] = cp.go(slot(r, 2, 0, c), slot(r, 2, 1, c), qdev)
        w_s[r, 2, 0] = cp.go(slot(r, 2, 0, c), slot(r, 2, 0, c), sib)

    def s3(r):
        for dz in (0, 3, 1, 2):
            w_x[r, dz].wait_recv()
            w_s[r, dz, 1] = cp.go(slot(r, dz, 1, c), slot(r, dz, 1, c), sib)

    def s4(r):
        for dz in (0, 3, 1, 2):
            for s in range(2):
                w_s[r, dz, s].wait_recv()

    for r in range(ROUNDS):
        w_load[r].wait()
        if r < OWN_Z:
            own_z(r)
        if r < OWN_X:
            own_x(r)
    for r in range(ROUNDS):
        own_s(r)

    a_copy = []
    for a in range(4):
        for copy in gh_load[a]:
            copy.wait()

        def up(j, _, a=a):
            rows = pl.ds(a * 128 + j * 16, 16)
            g = gv[rows].astype(F32)
            h = hv[rows].astype(F32)
            a_own[rows] = (h * (g / (1.0 + jnp.exp(-g)))).astype(BF16)
            return 0

        lax.fori_loop(0, 8, up, 0)
        rows = pl.ds(a * 128, 128)
        a_copy.append(cp.go(a_own.at[rows], a_pair.at[rows], pair))

    for copy in low_load:
        copy.wait()
    for n in range(4):
        rows = pl.ds(n * 128, 128)
        one = lax.dot_general(xv[rows], piv[...], LAST, preferred_element_type=F32)
        two = lax.dot_general(a_own[rows], pov[...], LAST, preferred_element_type=F32)
        both = jnp.concatenate([one, two], axis=1)
        low[(2 * n) % 4, n // 2] = both[:64]
        low[(2 * n + 1) % 4, n // 2] = both[64:]
    lc = {"a": [cp.go(low.at[(y + d) % 4], lowr.at[d - 1], y_dev[d]) for d in (1, 2, 3)]}

    def l2():
        for copy in lc["a"]:
            copy.wait_recv()
        lowz[0] = low[y, 1 - zl] + lowr[0, 1 - zl] + lowr[1, 1 - zl] + lowr[2, 1 - zl]
        lc["b"] = cp.go(lowz.at[0], lowz.at[1], zlp)
        lowz[2] = low[y, zl] + lowr[0, zl] + lowr[1, zl] + lowr[2, zl]

    def l3():
        lc["b"].wait_recv()
        total = lowz[1] + lowz[2]
        lane = lax.broadcasted_iota(jnp.int32, (64, 128), 1)
        out2 = jnp.where(lane < 64, pltpu.roll(total, 64, 1), total)
        local = ids_ref[...] - 4 * e + 4 * c
        hot = (lax.broadcasted_iota(jnp.int32, (8, 512), 0) == local).astype(F32)
        hot = pltpu.roll(hot, (8 - t) % 8 * 64, 1)[:, :64] * ((4 / 512) ** 0.5)
        sides = jnp.concatenate([total, jnp.zeros((64, 128), F32)], axis=0).T[:64, :64]
        left = (sides[:, None, :] * hot[None, :, :]).reshape(512, 64)
        grads = jnp.dot(left, out2, precision=HIGHEST, preferred_element_type=F32).reshape(64, 8, 128)
        low_half = lax.broadcasted_iota(jnp.int32, (8, 128), 1) < 64
        for j in range(32):
            part = jnp.where(low_half, grads[2 * j], grads[2 * j + 1])
            fpart[(j // 4) % 4, j // 16, :, (j % 4) * 128 : (j % 4) * 128 + 128] = part
        lc["c"] = [cp.go(fpart.at[(y + d) % 4], fpr.at[d - 1], y_dev[d]) for d in (1, 2, 3)]

    def l4():
        for copy in lc["c"]:
            copy.wait_recv()
        oth = 1 - zl
        fz[0] = fpart[y, oth] + fpr[0, oth] + fpr[1, oth] + fpr[2, oth]
        lc["d"] = cp.go(fz.at[0], fz.at[1], zlp)
        fz[2] = fpart[y, zl] + fpr[0, zl] + fpr[1, zl] + fpr[2, zl]

    def l5():
        lc["d"].wait_recv()
        mine = fz[1] + fz[2]
        halves = [jnp.concatenate([mine[:, q : q + 128], mine[:, q + 128 : q + 256]], axis=0) for q in (0, 256)]
        keep = jnp.where(c == 0, halves[0], halves[1])
        fsib[0] = jnp.where(c == 0, halves[1], halves[0])
        fsib[2] = keep
        lc["sib"] = cp.go(fsib.at[0], fsib.at[1], sib)
        feat_ref[y, zl] = mine
        lc["o1"] = cp.go(feat_ref.at[y, zl], feat_ref.at[y, zl], zlp)

    def l6():
        lc["sib"].wait_recv()
        gcol[c, 0, 0] = (fsib[1] + fsib[2]).astype(BF16)
        lc["x"] = [cp.go(gcol.at[c, 0, 0], gcol.at[c, 0, dx], xs_dev[dx]) for dx in (1, 2, 3)]
        lc["o1"].wait_recv()
        lc["out"] = [cp.go(feat_ref.at[y], feat_ref.at[y], y_dev[d]) for d in (1, 2, 3)]

    def l7():
        for copy in lc["x"]:
            copy.wait_recv()
        lc["z"] = [cp.go(gcol.at[c, 0], gcol.at[c, dz], zs_dev[dz]) for dz in (1, 2, 3)]

    def l8():
        for copy in lc["z"]:
            copy.wait_recv()
        lc["half"] = cp.go(gcol.at[c], gcol.at[c], sib)

    def l9():
        lc["half"].wait_recv()
        both = gcol[(e // 2) % 2].astype(F32)
        first = both[:, :, :8].reshape(128, 128)
        rowb[0] = jnp.where(e % 2 == 0, first, both[:, :, 8:].reshape(128, 128)).astype(BF16)
        index = cp.count
        cp.count += 8
        lc["row"] = [
            pltpu.make_async_remote_copy(
                src_ref=rowb.at[0],
                dst_ref=rowb.at[1],
                send_sem=send_sems.at[index + i],
                recv_sem=recv_sems.at[index],
                device_id=(e, tidx[d]),
                device_id_type=MESH,
            )
            for i, d in enumerate(tens)
        ]

        @pl.when(t == e // 4)
        def _():
            for copy in lc["row"]:
                copy.start()
            rowb[1] = rowb[0]

    def la():
        @pl.when(t == e // 4)
        def _():
            for copy in lc["row"]:
                copy.wait_send()

        @pl.when(t != e // 4)
        def _():
            lc["row"][0].wait_recv()

    def kslot(yy):
        return ((yy // 2 + zh) % 2) * 2 + (yy % 2 + x // 2) % 2

    k0, kp, km, k2 = (kslot((y + d) % 4) for d in (0, 1, 3, 2))
    base = ((zh + k0 // 2) % 4) // 2
    h_own = (zl + base) % 2
    h_oth = 1 - h_own
    par = (y + x // 2 + x) % 2
    off = [sum(NT[:i]) for i in range(NB)]
    poff = [sum(NP[:i]) for i in range(NB)]
    c1c, c2c, zc, xc = {}, {}, {}, {}

    def mm(w, a_ref, rows):
        return lax.dot_general(w, a_ref[rows], LAST, preferred_element_type=F32)

    def put(res, n):
        for k in range(4):
            for h in range(2):
                row0 = (k * 2 + h) * SUB
                sb[k, h, n] = res[row0 : row0 + SUB].astype(BF16)

    waited = set()

    def compute(i):
        w = {}
        tiles = BATCHES[i]
        n = 0
        while n < len(tiles):
            kind, r, chunk = tiles[n]
            if kind == "pair" and chunk not in waited:
                waited.add(chunk)
                a_copy[chunk].wait_recv()
            wide = 2 if n + 1 < len(tiles) and tiles[n + 1] == (kind, r, chunk + 1) and chunk % 2 == 0 else 1
            if wide == 2 and kind == "pair" and chunk + 1 not in waited:
                waited.add(chunk + 1)
                a_copy[chunk + 1].wait_recv()
            src = a_own if kind == "own" else a_pair
            res = mm(wbuf[r].reshape(16 * ROWS, KDIM), src, pl.ds(chunk * 128, 128 * wide))
            for q in range(wide):
                put(res[:, q * 128 : q * 128 + 128], off[i] + n + q)
            n += wide

    def c1(i):
        span = pl.ds(off[i], NT[i])
        c1c[i, "p"] = cp.go(sb.at[k2, 0, span], r1p.at[span], yp)
        c1c[i, "m"] = cp.go(sb.at[k2, 1, span], r1m.at[span], ym)
        c2c[i, "p1"] = cp.go(sb.at[kp, 1, span], r2m.at[1, span], yp)
        c2c[i, "m0"] = cp.go(sb.at[km, 0, span], r2p.at[0, span], ym)

    def c2(i):
        span = pl.ds(off[i], NT[i])
        c1c[i, "p"].wait_recv()
        sb[kp, 0, span] = (sb[kp, 0, span].astype(F32) + r1p[span].astype(F32)).astype(BF16)
        c2c[i, "p0"] = cp.go(sb.at[kp, 0, span], r2m.at[0, span], yp)
        c1c[i, "m"].wait_recv()
        sb[km, 1, span] = (sb[km, 1, span].astype(F32) + r1m[span].astype(F32)).astype(BF16)
        c2c[i, "m1"] = cp.go(sb.at[km, 1, span], r2p.at[1, span], ym)

    def c3(i):
        span = pl.ds(off[i], NT[i])
        for name in ("p1", "m0", "p0", "m1"):
            c2c[i, name].wait_recv()

        def total(h, span):
            return sb[k0, h, span].astype(F32) + r2m[h, span].astype(F32) + r2p[h, span].astype(F32)

        if i < LATE:
            zs[span] = total(h_oth, span).astype(BF16)
            zc[i] = cp.go(zs.at[span], zr.at[span], zlp)
            sown[span] = total(h_own, span)
            return
        owns = len(OWNS[i])
        osrc, psrc = pl.ds(off[i], owns), pl.ds(off[i] + owns, NP[i])
        pspan, lspan = pl.ds(poff[i], NP[i]), pl.ds(poff[i] - poff[LATE], NP[i])
        zs[psrc] = total(h_oth, psrc).astype(BF16)
        xc[i, 2] = cp.go(zs.at[psrc], xr2.at[lspan], pairz)
        zs[osrc] = total(h_oth, osrc).astype(BF16)
        zc[i] = cp.go(zs.at[osrc], zr.at[osrc], zlp)
        xs[pspan] = total(h_own, psrc).astype(BF16)
        xc[i] = cp.go(xs.at[pspan], xr.at[pspan], pair)
        sown[osrc] = total(h_own, osrc)

    def c4(i):
        owns = len(OWNS[i])
        zc[i].wait_recv()
        if NP[i] and i < LATE:
            src = pl.ds(off[i] + owns, NP[i])
            span = pl.ds(poff[i], NP[i])
            xs[span] = (sown[src] + zr[src].astype(F32)).astype(BF16)
            xc[i] = cp.go(xs.at[span], xr.at[span], pair)
        for n, (_, r, a) in enumerate(OWNS[i]):
            done = (sown[off[i] + n] + zr[off[i] + n].astype(F32)).astype(BF16)
            o_ref[par, 0, r, :, a * 128 : a * 128 + 128] = done[:ROWS]
            o_ref[par, 1, r, :, a * 128 : a * 128 + 128] = done[ROWS:]

    def c5(i):
        if NP[i]:
            xc[i].wait_recv()
        if i >= LATE:
            xc[i, 2].wait_recv()
        for n, (_, r, a) in enumerate(PAIRS[i]):
            done = xr[poff[i] + n]
            if i >= LATE:
                more = xr2[poff[i] - poff[LATE] + n]
                done = (done.astype(F32) + more.astype(F32)).astype(BF16)
            o_ref[1 - par, 0, r, :, a * 128 : a * 128 + 128] = done[:ROWS]
            o_ref[1 - par, 1, r, :, a * 128 : a * 128 + 128] = done[ROWS:]

    table = {
        "s1": s1, "s2": s2, "s3": s3, "s4": s4, "mm": compute,
        "c1": c1, "c2": c2, "c3": c3, "c4": c4, "c5": c5,
        "l3": l3, "l4": l4, "l5": l5, "l6": l6, "l7": l7, "l8": l8, "l9": l9, "la": la, "l2": l2,
    }
    for step in STEPS:
        if step[0] == "l":
            table[step]()
        else:
            table[step[:2]](int(step[2:]))
    for copy in lc["out"]:
        copy.wait_recv()
    for copy in cp.sent:
        copy.wait_send()


def finish(o_ref, feat_ref, gcol, rowb, grad_ref, out_ref, hess_ref):
    e = lax.axis_index("example")
    t = lax.axis_index("tensor")
    for q in range(4):
        rows = slice(q * 128, q * 128 + 128)
        grad_ref[:, rows] = o_ref[rows].astype(F32).T.astype(BF16)
    for yy in range(4):
        for zz in range(2):
            both = feat_ref[yy, zz]
            first = (zz * 4 + yy) * 512
            out_ref[:, first : first + 512] = both[:4] + both[4:]
    parts = []
    for q in range(4):
        part = gcol[q // 2, :, :, (q % 2) * 8 : (q % 2) * 8 + 8]
        parts.append(part.astype(F32).reshape(128, 128))
    col = jnp.concatenate(parts, axis=1).astype(BF16)
    gram = jnp.dot(rowb[1].astype(F32).T.astype(BF16), col, preferred_element_type=F32) / 128.0
    rg = lax.broadcasted_iota(jnp.int32, (128, 512), 0) + e * 128
    cg = lax.broadcasted_iota(jnp.int32, (128, 512), 1) + t * 512
    hess_ref[...] = gram + DAMPING * (rg == cg).astype(F32)


def body(layer_input, gate_act, hidden_grad, up_weight, proj_input, proj_output, sequence_ids):
    tiles = sum(NT)
    pair_tiles = sum(NP)
    anyspec = pl.BlockSpec(memory_space=pl.ANY)
    vm = pl.BlockSpec(memory_space=pltpu.VMEM)
    o, feat, gcol, rowb = pl.pallas_call(
        kernel,
        out_shape=(
            jax.ShapeDtypeStruct((2, 2, ROUNDS, ROWS, TOK), BF16),
            jax.ShapeDtypeStruct((4, 2, 8, 512), F32),
            jax.ShapeDtypeStruct((2, 4, 4, 16, 128), BF16),
            jax.ShapeDtypeStruct((2, 128, 128), BF16),
        ),
        in_specs=[anyspec] * 6 + [vm],
        out_specs=(vm, vm, vm, vm),
        scratch_shapes=[
            pltpu.VMEM((512, 512), BF16),
            pltpu.VMEM((512, KDIM), BF16),
            pltpu.VMEM((512, KDIM), BF16),
            pltpu.VMEM((RANK, 512), BF16),
            pltpu.VMEM((RANK, KDIM), BF16),
            pltpu.VMEM((512, KDIM), BF16),
            pltpu.VMEM((512, KDIM), BF16),
            pltpu.VMEM((ROUNDS, 4, 4, ROWS, KDIM), BF16),
        ]
        + [pltpu.VMEM((4, 2, tiles, SUB, 128), BF16)]
        + [
            pltpu.VMEM((tiles, SUB, 128), BF16),
            pltpu.VMEM((tiles, SUB, 128), BF16),
            pltpu.VMEM((2, tiles, SUB, 128), BF16),
            pltpu.VMEM((2, tiles, SUB, 128), BF16),
            pltpu.VMEM((tiles, SUB, 128), BF16),
            pltpu.VMEM((tiles, SUB, 128), BF16),
            pltpu.VMEM((tiles, SUB, 128), F32),
            pltpu.VMEM((pair_tiles, SUB, 128), BF16),
            pltpu.VMEM((pair_tiles, SUB, 128), BF16),
            pltpu.VMEM((sum(NP[LATE:]), SUB, 128), BF16),
            pltpu.VMEM((4, 2, 64, 128), F32),
            pltpu.VMEM((3, 2, 64, 128), F32),
            pltpu.VMEM((3, 64, 128), F32),
            pltpu.VMEM((4, 2, 8, 512), F32),
            pltpu.VMEM((3, 2, 8, 512), F32),
            pltpu.VMEM((3, 8, 512), F32),
            pltpu.VMEM((3, 16, 128), F32),
            pltpu.SemaphoreType.DMA((N_COPIES,)),
            pltpu.SemaphoreType.DMA((N_COPIES,)),
            pltpu.SemaphoreType.DMA((24,)),
        ],
        compiler_params=pltpu.CompilerParams(
            collective_id=0, has_side_effects=True, vmem_limit_bytes=60 * 1024 * 1024
        ),
    )(layer_input, gate_act, hidden_grad, up_weight, proj_input.T, proj_output.T, sequence_ids.reshape(1, 512))
    return pl.pallas_call(
        finish,
        out_shape=(
            jax.ShapeDtypeStruct((TOK, 512), BF16),
            jax.ShapeDtypeStruct((4, 4096), F32),
            jax.ShapeDtypeStruct((128, 512), F32),
        ),
        in_specs=[vm] * 4,
        out_specs=(vm, vm, vm),
    )(o.reshape(512, TOK), feat, gcol, rowb)


def solution(mesh):
    return jax.shard_map(
        body,
        mesh=mesh,
        in_specs=(
            P("example", "tensor"),
            P("example", "tensor"),
            P("example", "tensor"),
            P("example", "tensor"),
            P("tensor", None),
            P("tensor", None),
            P("example"),
        ),
        out_specs=(P("example", "tensor"), P("example", None), P("example", "tensor")),
        check_vma=False,
    )
```

```python
import jax
import jax.numpy as jnp
from jax import lax
from jax.experimental import pallas as pl
from jax.experimental.pallas import tpu as pltpu
from jax.sharding import PartitionSpec as P

MESH = pl.DeviceIdType.MESH
F32 = jnp.float32
BF16 = jnp.bfloat16
LAST = (((1,), (1,)), ((), ()))
HIGHEST = lax.Precision.HIGHEST

DAMPING = 0.1
TOK = 512
KDIM = 1792
RANK = 64
ROUNDS = 8
ROWS = 16
SUB = 2 * ROWS
OWN_X, OWN_Z = 4, 3
PLAN = (
    ("0o", "00"),
    ("1o", "10"),
    ("2o", "20", "21", "01", "11"),
    ("3o", "30", "31"),
    ("4o", "40", "41", "42", "02", "12", "22", "32"),
    ("5o", "50", "51", "52"),
    ("03", "13", "23", "33", "43", "53"),
    ("6o", "60", "61", "62", "63"),
    ("70", "71", "72", "73"),
    ("7o",),
)


def tiles_of(text):
    own, other = [], []
    for word in text:
        if word[1] == "o":
            own += [("own", int(word[0]), n) for n in range(4)]
        else:
            other.append(("pair", int(word[0]), int(word[1])))
    return own, other


OWNS = [tiles_of(text)[0] for text in PLAN]
PAIRS = [tiles_of(text)[1] for text in PLAN]
BATCHES = [o + p for o, p in zip(OWNS, PAIRS)]
NB = len(BATCHES)
LATE = 8
NT = [len(q) for q in BATCHES]
NP = [len(q) for q in PAIRS]

STEPS = (
    "s10", "s11", "s20", "s12", "l2", "s30", "s21", "s40", "mm0", "c10", "s13", "l3",
    "s31", "s22", "s14", "s41", "mm1", "c11", "c20", "l4", "s32", "s23", "s15", "s42",
    "mm2", "c12", "c21", "l5", "s33", "s24", "s16", "s43", "mm3", "c13", "c22", "c30",
    "l6", "s34", "s25", "s17", "s44", "mm4", "c14", "c23", "c31", "l7", "s26", "s35",
    "s45", "mm5", "c15", "c24", "c32", "l8", "s27", "mm6", "c16", "c25", "c33", "c40",
    "c41", "s36", "s46", "mm7", "c17", "c26", "c34", "c42", "c43", "l9", "s37", "c35",
    "c44", "s47", "mm8", "c18", "mm9", "c27", "c19", "c36", "c45", "c28", "c37", "c46",
    "c29", "c38", "c47", "c39", "c50", "c51", "c52", "c53", "c54", "c55", "c56", "c57",
    "c49", "la", "c58",
)


class Copies:
    def __init__(self, send_sems, recv_sems):
        self.send, self.recv, self.count, self.sent = send_sems, recv_sems, 0, []

    def make(self, src, dst, device):
        index = self.count
        self.count += 1
        copy = pltpu.make_async_remote_copy(
            src_ref=src,
            dst_ref=dst,
            send_sem=self.send.at[index],
            recv_sem=self.recv.at[index],
            device_id=device,
            device_id_type=MESH,
        )
        return copy

    def go(self, src, dst, device):
        copy = self.make(src, dst, device)
        copy.start()
        self.sent.append(copy)
        return copy


N_COPIES = 300


def kernel(
    x_in, gate_in, hid_in, w_in, pi_in, po_in, ids_ref,
    o_ref, feat_ref, gcol, rowb,
    xv, gv, hv, piv, pov, a_own, a_pair, wbuf,
    sb, r1p, r1m, r2m, r2p, zs, zr, sown, xs, xr, xr2,
    low, lowr, lowz, fpart, fpr, fz, fsib,
    send_sems, recv_sems, loc_sems,
):
    e = lax.axis_index("example")
    t = lax.axis_index("tensor")
    zh, x, c = e // 8, (e // 2) % 4, e % 2
    zl, y = t // 4, t % 4

    def ex(zh_, x_, c_):
        return zh_ * 8 + x_ * 2 + c_

    def te(zl_, y_):
        return zl_ * 4 + y_

    sib = (ex(zh, x, 1 - c), t)
    pair = (ex(zh, x + 1 - 2 * (x % 2), c), t)
    pairz = (ex(zh, x + 1 - 2 * (x % 2), c), te(1 - zl, y))
    qdev = (ex(zh, 3 - x, c), t)
    zp = (ex((zh + 1) % 4, x, c), t)
    zm = (ex((zh + 3) % 4, x, c), t)
    yp = (e, te(zl, (y + 1) % 4))
    ym = (e, te(zl, (y + 3) % 4))
    zlp = (e, te(1 - zl, y))
    xs_dev = {dx: (ex(zh, (x + dx) % 4, c), t) for dx in (1, 2, 3)}
    zs_dev = {dz: (ex((zh + dz) % 4, x, c), t) for dz in (1, 2, 3)}
    y_dev = {d: (e, te(zl, (y + d) % 4)) for d in (1, 2, 3)}
    tens = [(dzl, dy) for dzl in range(2) for dy in range(4) if (dzl, dy) != (0, 0)]
    tidx = {d: te((zl + d[0]) % 2, (y + d[1]) % 4) for d in tens}

    barrier = pltpu.get_barrier_semaphore()
    partners = [sib, pairz] + list(xs_dev.values()) + list(zs_dev.values()) + [(e, tidx[d]) for d in tens]
    for dev in partners:
        pl.semaphore_signal(barrier, inc=1, device_id=dev, device_id_type=MESH)

    loads = []

    def load(src, dst):
        copy = pltpu.make_async_copy(src, dst, loc_sems.at[len(loads)])
        copy.start()
        loads.append(copy)
        return copy

    w_load = [load(w_in.at[pl.ds(r * ROWS, ROWS)], wbuf.at[r, 0, 0, c]) for r in range(ROUNDS)]
    gh_load = []
    for a in range(4):
        rows = pl.ds(a * 128, 128)
        gh_load.append((load(gate_in.at[rows], gv.at[rows]), load(hid_in.at[rows], hv.at[rows])))
    low_load = [load(x_in, xv), load(pi_in, piv), load(po_in, pov)]

    pl.semaphore_wait(barrier, len(partners))
    cp = Copies(send_sems, recv_sems)

    def slot(r, dz, s, core):
        return wbuf.at[r, (dz % 2) * 2 + s, dz // 2, core]

    def slots(r, dz, s, core):
        return wbuf.at[r, dz * 2 + s, :, core]

    w_z = {}
    w_x = {}
    w_s = {}

    def own_z(r):
        if r < ROUNDS:
            w_z[r, 3] = cp.go(slot(r, 0, 0, c), slot(r, 3, 0, c), zp)
            w_z[r, 1] = cp.go(slot(r, 0, 0, c), slot(r, 1, 0, c), zm)

    def own_x(r):
        if r < ROUNDS:
            w_x[r, 0] = cp.go(slot(r, 0, 0, c), slot(r, 0, 1, c), qdev)

    def s1(r):
        w_z[r, 3].wait_recv()
        if r % 2 == 0:
            w_z[r, 2] = cp.go(slot(r, 3, 0, c), slot(r, 2, 0, c), zp)
        w_z[r, 1].wait_recv()
        if r % 2 == 1:
            w_z[r, 2] = cp.go(slot(r, 1, 0, c), slot(r, 2, 0, c), zm)
        own_z(r + OWN_Z)
        w_x[r, 1] = cp.go(slots(r, 1, 0, c), slots(r, 1, 1, c), qdev)
        own_x(r + OWN_X)
        w_s[r, 1, 0] = cp.go(slots(r, 1, 0, c), slots(r, 1, 0, c), sib)

    def s2(r):
        w_z[r, 2].wait_recv()
        w_x[r, 2] = cp.go(slot(r, 2, 0, c), slot(r, 2, 1, c), qdev)
        w_s[r, 0, 0] = cp.go(slots(r, 0, 0, c), slots(r, 0, 0, c), sib)

    def s3(r):
        w_x[r, 1].wait_recv()
        w_s[r, 1, 1] = cp.go(slots(r, 1, 1, c), slots(r, 1, 1, c), sib)
        w_x[r, 0].wait_recv()
        w_x[r, 2].wait_recv()
        w_s[r, 0, 1] = cp.go(slots(r, 0, 1, c), slots(r, 0, 1, c), sib)

    def s4(r):
        for dz in (1, 0):
            for s in range(2):
                w_s[r, dz, s].wait_recv()

    for r in range(ROUNDS):
        w_load[r].wait()
        if r < OWN_Z:
            own_z(r)
        if r < OWN_X:
            own_x(r)

    a_copy = []
    for a in range(4):
        for copy in gh_load[a]:
            copy.wait()

        def up(j, _, a=a):
            rows = pl.ds(a * 128 + j * 16, 16)
            g = gv[rows].astype(F32)
            h = hv[rows].astype(F32)
            a_own[rows] = (h * (g / (1.0 + jnp.exp(-g)))).astype(BF16)
            return 0

        lax.fori_loop(0, 8, up, 0)
        rows = pl.ds(a * 128, 128)
        a_copy.append(cp.go(a_own.at[rows], a_pair.at[rows], pair))

    for copy in low_load:
        copy.wait()
    for n in range(4):
        rows = pl.ds(n * 128, 128)
        one = lax.dot_general(xv[rows], piv[...], LAST, preferred_element_type=F32)
        two = lax.dot_general(a_own[rows], pov[...], LAST, preferred_element_type=F32)
        both = jnp.concatenate([one, two], axis=1)
        low[(2 * n) % 4, n // 2] = both[:64]
        low[(2 * n + 1) % 4, n // 2] = both[64:]
    lc = {"a": [cp.go(low.at[(y + d) % 4], lowr.at[d - 1], y_dev[d]) for d in (1, 2, 3)]}

    def l2():
        for copy in lc["a"]:
            copy.wait_recv()
        lowz[0] = low[y, 1 - zl] + lowr[0, 1 - zl] + lowr[1, 1 - zl] + lowr[2, 1 - zl]
        lc["b"] = cp.go(lowz.at[0], lowz.at[1], zlp)
        lowz[2] = low[y, zl] + lowr[0, zl] + lowr[1, zl] + lowr[2, zl]

    def l3():
        lc["b"].wait_recv()
        total = lowz[1] + lowz[2]
        lane = lax.broadcasted_iota(jnp.int32, (64, 128), 1)
        out2 = jnp.where(lane < 64, pltpu.roll(total, 64, 1), total)
        local = ids_ref[...] - 4 * e + 4 * c
        hot = (lax.broadcasted_iota(jnp.int32, (8, 512), 0) == local).astype(F32)
        hot = pltpu.roll(hot, (8 - t) % 8 * 64, 1)[:, :64] * ((4 / 512) ** 0.5)
        sides = jnp.concatenate([total, jnp.zeros((64, 128), F32)], axis=0).T[:64, :64]
        left = (sides[:, None, :] * hot[None, :, :]).reshape(512, 64)
        grads = jnp.dot(left, out2, precision=HIGHEST, preferred_element_type=F32).reshape(64, 8, 128)
        low_half = lax.broadcasted_iota(jnp.int32, (8, 128), 1) < 64
        for j in range(32):
            part = jnp.where(low_half, grads[2 * j], grads[2 * j + 1])
            fpart[(j // 4) % 4, j // 16, :, (j % 4) * 128 : (j % 4) * 128 + 128] = part
        lc["c"] = [cp.go(fpart.at[(y + d) % 4], fpr.at[d - 1], y_dev[d]) for d in (1, 2, 3)]

    def l4():
        for copy in lc["c"]:
            copy.wait_recv()
        oth = 1 - zl
        fz[0] = fpart[y, oth] + fpr[0, oth] + fpr[1, oth] + fpr[2, oth]
        lc["d"] = cp.go(fz.at[0], fz.at[1], zlp)
        fz[2] = fpart[y, zl] + fpr[0, zl] + fpr[1, zl] + fpr[2, zl]

    def l5():
        lc["d"].wait_recv()
        mine = fz[1] + fz[2]
        halves = [jnp.concatenate([mine[:, q : q + 128], mine[:, q + 128 : q + 256]], axis=0) for q in (0, 256)]
        keep = jnp.where(c == 0, halves[0], halves[1])
        fsib[0] = jnp.where(c == 0, halves[1], halves[0])
        fsib[2] = keep
        lc["sib"] = cp.go(fsib.at[0], fsib.at[1], sib)
        feat_ref[y, zl] = mine
        lc["o1"] = cp.go(feat_ref.at[y, zl], feat_ref.at[y, zl], zlp)

    def l6():
        lc["sib"].wait_recv()
        gcol[c, 0, 0] = (fsib[1] + fsib[2]).astype(BF16)
        lc["x"] = [cp.go(gcol.at[c, 0, 0], gcol.at[c, 0, dx], xs_dev[dx]) for dx in (1, 2, 3)]
        lc["o1"].wait_recv()
        lc["out"] = [cp.go(feat_ref.at[y], feat_ref.at[y], y_dev[d]) for d in (1, 2, 3)]

    def l7():
        for copy in lc["x"]:
            copy.wait_recv()
        lc["z"] = [cp.go(gcol.at[c, 0], gcol.at[c, dz], zs_dev[dz]) for dz in (1, 2, 3)]

    def l8():
        for copy in lc["z"]:
            copy.wait_recv()
        lc["half"] = cp.go(gcol.at[c], gcol.at[c], sib)

    def l9():
        lc["half"].wait_recv()
        both = gcol[(e // 2) % 2].astype(F32)
        first = both[:, :, :8].reshape(128, 128)
        rowb[0] = jnp.where(e % 2 == 0, first, both[:, :, 8:].reshape(128, 128)).astype(BF16)
        index = cp.count
        cp.count += 8
        lc["row"] = [
            pltpu.make_async_remote_copy(
                src_ref=rowb.at[0],
                dst_ref=rowb.at[1],
                send_sem=send_sems.at[index + i],
                recv_sem=recv_sems.at[index],
                device_id=(e, tidx[d]),
                device_id_type=MESH,
            )
            for i, d in enumerate(tens)
        ]

        @pl.when(t == e // 4)
        def _():
            for copy in lc["row"]:
                copy.start()
            rowb[1] = rowb[0]

    def la():
        @pl.when(t == e // 4)
        def _():
            for copy in lc["row"]:
                copy.wait_send()

        @pl.when(t != e // 4)
        def _():
            lc["row"][0].wait_recv()

    def kslot(yy):
        return ((yy // 2 + zh) % 2) * 2 + (yy % 2 + x // 2) % 2

    k0, kp, km, k2 = (kslot((y + d) % 4) for d in (0, 1, 3, 2))
    base = ((zh + k0 // 2) % 4) // 2
    h_own = (zl + base) % 2
    h_oth = 1 - h_own
    par = (y + x // 2 + x) % 2
    off = [sum(NT[:i]) for i in range(NB)]
    poff = [sum(NP[:i]) for i in range(NB)]
    c1c, c2c, zc, xc = {}, {}, {}, {}

    def mm(w, a_ref, rows):
        return lax.dot_general(w, a_ref[rows], LAST, preferred_element_type=F32)

    def put(res, n):
        for k in range(4):
            for h in range(2):
                row0 = (k * 2 + h) * SUB
                sb[k, h, n] = res[row0 : row0 + SUB].astype(BF16)

    waited = set()

    def compute(i):
        w = {}
        tiles = BATCHES[i]
        n = 0
        while n < len(tiles):
            kind, r, chunk = tiles[n]
            if kind == "pair" and chunk not in waited:
                waited.add(chunk)
                a_copy[chunk].wait_recv()
            wide = 2 if n + 1 < len(tiles) and tiles[n + 1] == (kind, r, chunk + 1) and chunk % 2 == 0 else 1
            if wide == 2 and kind == "pair" and chunk + 1 not in waited:
                waited.add(chunk + 1)
                a_copy[chunk + 1].wait_recv()
            src = a_own if kind == "own" else a_pair
            res = mm(wbuf[r].reshape(16 * ROWS, KDIM), src, pl.ds(chunk * 128, 128 * wide))
            for q in range(wide):
                put(res[:, q * 128 : q * 128 + 128], off[i] + n + q)
            n += wide

    def c1(i):
        span = pl.ds(off[i], NT[i])
        c1c[i, "p"] = cp.go(sb.at[k2, 0, span], r1p.at[span], yp)
        c1c[i, "m"] = cp.go(sb.at[k2, 1, span], r1m.at[span], ym)
        c2c[i, "p1"] = cp.go(sb.at[kp, 1, span], r2m.at[1, span], yp)
        c2c[i, "m0"] = cp.go(sb.at[km, 0, span], r2p.at[0, span], ym)

    def c2(i):
        span = pl.ds(off[i], NT[i])
        c1c[i, "p"].wait_recv()
        sb[kp, 0, span] = (sb[kp, 0, span].astype(F32) + r1p[span].astype(F32)).astype(BF16)
        c2c[i, "p0"] = cp.go(sb.at[kp, 0, span], r2m.at[0, span], yp)
        c1c[i, "m"].wait_recv()
        sb[km, 1, span] = (sb[km, 1, span].astype(F32) + r1m[span].astype(F32)).astype(BF16)
        c2c[i, "m1"] = cp.go(sb.at[km, 1, span], r2p.at[1, span], ym)

    def c3(i):
        span = pl.ds(off[i], NT[i])
        for name in ("p1", "m0", "p0", "m1"):
            c2c[i, name].wait_recv()

        def total(h, span):
            return sb[k0, h, span].astype(F32) + r2m[h, span].astype(F32) + r2p[h, span].astype(F32)

        if i < LATE:
            zs[span] = total(h_oth, span).astype(BF16)
            zc[i] = cp.go(zs.at[span], zr.at[span], zlp)
            sown[span] = total(h_own, span)
            return
        owns = len(OWNS[i])
        osrc, psrc = pl.ds(off[i], owns), pl.ds(off[i] + owns, NP[i])
        pspan, lspan = pl.ds(poff[i], NP[i]), pl.ds(poff[i] - poff[LATE], NP[i])
        if NP[i]:
            zs[psrc] = total(h_oth, psrc).astype(BF16)
            xc[i, 2] = cp.go(zs.at[psrc], xr2.at[lspan], pairz)
            xs[pspan] = total(h_own, psrc).astype(BF16)
            xc[i] = cp.go(xs.at[pspan], xr.at[pspan], pair)
        if owns:
            zs[osrc] = total(h_oth, osrc).astype(BF16)
            zc[i] = cp.go(zs.at[osrc], zr.at[osrc], zlp)
            sown[osrc] = total(h_own, osrc)

    def c4(i):
        owns = len(OWNS[i])
        if owns or i < LATE:
            zc[i].wait_recv()
        if NP[i] and i < LATE:
            src = pl.ds(off[i] + owns, NP[i])
            span = pl.ds(poff[i], NP[i])
            xs[span] = (sown[src] + zr[src].astype(F32)).astype(BF16)
            xc[i] = cp.go(xs.at[span], xr.at[span], pair)
        for n, (_, r, a) in enumerate(OWNS[i]):
            done = (sown[off[i] + n] + zr[off[i] + n].astype(F32)).astype(BF16)
            o_ref[par, 0, r, :, a * 128 : a * 128 + 128] = done[:ROWS]
            o_ref[par, 1, r, :, a * 128 : a * 128 + 128] = done[ROWS:]

    def c5(i):
        if NP[i]:
            xc[i].wait_recv()
        if i >= LATE and NP[i]:
            xc[i, 2].wait_recv()
        for n, (_, r, a) in enumerate(PAIRS[i]):
            done = xr[poff[i] + n]
            if i >= LATE:
                more = xr2[poff[i] - poff[LATE] + n]
                done = (done.astype(F32) + more.astype(F32)).astype(BF16)
            o_ref[1 - par, 0, r, :, a * 128 : a * 128 + 128] = done[:ROWS]
            o_ref[1 - par, 1, r, :, a * 128 : a * 128 + 128] = done[ROWS:]

    table = {
        "s1": s1, "s2": s2, "s3": s3, "s4": s4, "mm": compute,
        "c1": c1, "c2": c2, "c3": c3, "c4": c4, "c5": c5,
        "l3": l3, "l4": l4, "l5": l5, "l6": l6, "l7": l7, "l8": l8, "l9": l9, "la": la, "l2": l2,
    }
    old = [0, 0]

    def settle():
        for copy in cp.sent[old[0] : old[1]]:
            copy.wait_send()
        old[0], old[1] = old[1], len(cp.sent)

    for step in STEPS:
        if step == "f":
            settle()
        elif step[0] == "l":
            table[step]()
        else:
            table[step[:2]](int(step[2:]))
    for copy in lc["out"]:
        copy.wait_recv()
    for copy in cp.sent[old[0] :]:
        copy.wait_send()


def finish(o_ref, feat_ref, gcol, rowb, grad_ref, out_ref, hess_ref):
    e = lax.axis_index("example")
    t = lax.axis_index("tensor")
    for q in range(4):
        rows = slice(q * 128, q * 128 + 128)
        grad_ref[:, rows] = o_ref[rows].astype(F32).T.astype(BF16)
    for yy in range(4):
        for zz in range(2):
            both = feat_ref[yy, zz]
            first = (zz * 4 + yy) * 512
            out_ref[:, first : first + 512] = both[:4] + both[4:]
    parts = []
    for q in range(4):
        part = gcol[q // 2, :, :, (q % 2) * 8 : (q % 2) * 8 + 8]
        parts.append(part.astype(F32).reshape(128, 128))
    col = jnp.concatenate(parts, axis=1).astype(BF16)
    gram = jnp.dot(rowb[1].astype(F32).T.astype(BF16), col, preferred_element_type=F32) / 128.0
    rg = lax.broadcasted_iota(jnp.int32, (128, 512), 0) + e * 128
    cg = lax.broadcasted_iota(jnp.int32, (128, 512), 1) + t * 512
    hess_ref[...] = gram + DAMPING * (rg == cg).astype(F32)


def body(layer_input, gate_act, hidden_grad, up_weight, proj_input, proj_output, sequence_ids):
    tiles = sum(NT)
    pair_tiles = sum(NP)
    anyspec = pl.BlockSpec(memory_space=pl.ANY)
    vm = pl.BlockSpec(memory_space=pltpu.VMEM)
    o, feat, gcol, rowb = pl.pallas_call(
        kernel,
        out_shape=(
            jax.ShapeDtypeStruct((2, 2, ROUNDS, ROWS, TOK), BF16),
            jax.ShapeDtypeStruct((4, 2, 8, 512), F32),
            jax.ShapeDtypeStruct((2, 4, 4, 16, 128), BF16),
            jax.ShapeDtypeStruct((2, 128, 128), BF16),
        ),
        in_specs=[anyspec] * 6 + [vm],
        out_specs=(vm, vm, vm, vm),
        scratch_shapes=[
            pltpu.VMEM((512, 512), BF16),
            pltpu.VMEM((512, KDIM), BF16),
            pltpu.VMEM((512, KDIM), BF16),
            pltpu.VMEM((RANK, 512), BF16),
            pltpu.VMEM((RANK, KDIM), BF16),
            pltpu.VMEM((512, KDIM), BF16),
            pltpu.VMEM((512, KDIM), BF16),
            pltpu.VMEM((ROUNDS, 4, 2, 2, ROWS, KDIM), BF16),
        ]
        + [pltpu.VMEM((4, 2, tiles, SUB, 128), BF16)]
        + [
            pltpu.VMEM((tiles, SUB, 128), BF16),
            pltpu.VMEM((tiles, SUB, 128), BF16),
            pltpu.VMEM((2, tiles, SUB, 128), BF16),
            pltpu.VMEM((2, tiles, SUB, 128), BF16),
            pltpu.VMEM((tiles, SUB, 128), BF16),
            pltpu.VMEM((tiles, SUB, 128), BF16),
            pltpu.VMEM((tiles, SUB, 128), F32),
            pltpu.VMEM((pair_tiles, SUB, 128), BF16),
            pltpu.VMEM((pair_tiles, SUB, 128), BF16),
            pltpu.VMEM((sum(NP[LATE:]), SUB, 128), BF16),
            pltpu.VMEM((4, 2, 64, 128), F32),
            pltpu.VMEM((3, 2, 64, 128), F32),
            pltpu.VMEM((3, 64, 128), F32),
            pltpu.VMEM((4, 2, 8, 512), F32),
            pltpu.VMEM((3, 2, 8, 512), F32),
            pltpu.VMEM((3, 8, 512), F32),
            pltpu.VMEM((3, 16, 128), F32),
            pltpu.SemaphoreType.DMA((N_COPIES,)),
            pltpu.SemaphoreType.DMA((N_COPIES,)),
            pltpu.SemaphoreType.DMA((24,)),
        ],
        compiler_params=pltpu.CompilerParams(
            collective_id=0, has_side_effects=True, vmem_limit_bytes=60 * 1024 * 1024
        ),
    )(layer_input, gate_act, hidden_grad, up_weight, proj_input.T, proj_output.T, sequence_ids.reshape(1, 512))
    return pl.pallas_call(
        finish,
        out_shape=(
            jax.ShapeDtypeStruct((TOK, 512), BF16),
            jax.ShapeDtypeStruct((4, 4096), F32),
            jax.ShapeDtypeStruct((128, 512), F32),
        ),
        in_specs=[vm] * 4,
        out_specs=(vm, vm, vm),
    )(o.reshape(512, TOK), feat, gcol, rowb)


def solution(mesh):
    return jax.shard_map(
        body,
        mesh=mesh,
        in_specs=(
            P("example", "tensor"),
            P("example", "tensor"),
            P("example", "tensor"),
            P("example", "tensor"),
            P("tensor", None),
            P("tensor", None),
            P("example"),
        ),
        out_specs=(P("example", "tensor"), P("example", None), P("example", "tensor")),
        check_vma=False,
    )
```
